32 devices in a mesh: blk: 8 (over z, y), lag: 4 (over x, core).
Axes of the slice: x: 2, y: 2, z: 4, core: 2. Of those that a mesh axis runs over, the one named last changes fastest.
Arguments:
- seismograms: float32 [1024, 3, 1024], P(('blk', 'lag')), may hold values from -70 to 70
- onset_shift: int32 [1024], P(('blk', 'lag')), may hold values from 0 to 63
- start_bits: int32 [1024], P(('blk', 'lag')), may hold values from 0 to 65535
Outputs:
- embedding: float32 [16, 1024], P(None, ('blk', 'lag'))
The draws below stay inside these ranges and needn't reach their ends.
Inputs may be any that keep to these rules, and one draw needn't show every extreme that they name: `start_bits`: bit k of an event's code is its entry in starting vector k.
All inputs are finite; a program needn't handle non-finite values.
Results may differ from the reference program's by a relative error of at most 0.0077.
Values may be sent and summed in bfloat16 or wider, within the bound.
A program may use at most 64 MiB of HBM per device.

```python
import jax
import jax.numpy as jnp
from jax import lax

COMPS = 3
SAMPLES = 1024
MAXLAG = 64
LAGS = 65
OFFMAX = 64
VECTORS = 16
ITERS = 3
BLOCK = 128
NBLOCKS = 8
EVENTS = 1024


def draw_seismograms(key, part):
    first_key = jax.random.fold_in(key, 0)
    shape = (EVENTS, COMPS, SAMPLES)
    return jnp.clip(jax.random.normal(first_key, shape, jnp.float32), -6.0, 6.0)


def with_ends(array, own_key, smallest, high):
    extent = array.shape
    place = [jax.random.randint(jax.random.fold_in(own_key, axis), (), 0, extent[axis]) for axis in range(len(extent))]
    array = array.at[tuple(place)].set(smallest)
    longest = extent.index(max(extent))
    place[longest] = (place[longest] + 1) % extent[longest]
    return array.at[tuple(place)].set(high)


def setup_inputs(seed: int = 0) -> dict:
    splits = jax.random.split(jax.random.key(seed), 4)
    return {
        "seismograms": draw_seismograms(jax.random.fold_in(splits[3], 71), 0),
        "onset_shift": with_ends(jax.random.randint(splits[1], (EVENTS,), 0, OFFMAX), jax.random.fold_in(splits[1], 1), 0, OFFMAX - 1).astype(jnp.int32),
        "start_bits": with_ends(jax.random.randint(splits[2], (EVENTS,), 0, 2 ** VECTORS), jax.random.fold_in(splits[2], 1), 0, (2 ** VECTORS) - 1).astype(jnp.int32),
    }


sharpness = 64.0

def align_unit(seismograms, onset_shift):
    padded = jnp.pad(seismograms, ((0, 0), (0, 0), (0, OFFMAX)))

    def slide(record, offset_at):
        return lax.dynamic_slice_in_dim(record, offset_at, SAMPLES, 1)
    aligned = jax.vmap(slide)(padded, onset_shift)
    energy = lax.optimization_barrier(jnp.sum(aligned * aligned, axis=(1, 2)))
    return (aligned * lax.rsqrt(energy + 1e-06)[:, None, None]).astype(jnp.bfloat16)

def block_affinity(centre, columns):
    padded = jnp.pad(centre, ((0, 0), (0, 0), (MAXLAG, MAXLAG)))
    row_count = centre.shape[0]

    def one_lag(running, lag_index):
        lag_value = 2 * lag_index - MAXLAG
        shifted = lax.dynamic_slice_in_dim(padded, MAXLAG - lag_value, SAMPLES, 2).reshape(row_count, -1)
        scores = jnp.dot(shifted.astype(jnp.float32), columns.T.astype(jnp.float32), preferred_element_type=jnp.float32)
        return (running + jnp.exp(sharpness * scores), None)
    start_sum = jnp.zeros((row_count, columns.shape[0]), jnp.float32)
    running, unused = lax.scan(one_lag, start_sum, jnp.arange(LAGS, dtype=jnp.int32))
    return running

def reference(seismograms, onset_shift, start_bits):

    def one_block(block_index):
        pieces = []
        for neighbour in (-1, 0, 1):
            first_row = ((block_index + neighbour) % NBLOCKS * BLOCK).astype(jnp.int32)
            pieces.append(align_unit(lax.dynamic_slice_in_dim(seismograms, first_row, BLOCK, 0), lax.dynamic_slice_in_dim(onset_shift, first_row, BLOCK, 0)))
        columns = jnp.concatenate(pieces, 0).reshape(3 * BLOCK, -1)
        band = block_affinity(pieces[1], columns)
        self_mask = jnp.arange(3 * BLOCK)[None, :] == (BLOCK + jnp.arange(BLOCK))[:, None]
        return jnp.where(self_mask, jnp.zeros_like(band), band)
    affinity = lax.map(one_block, jnp.arange(NBLOCKS, dtype=jnp.int32))
    degree = lax.optimization_barrier(jnp.sum(affinity, axis=2))
    degree_total = jnp.sum(degree)
    root_degree = jnp.sqrt(degree)
    inverse = lax.rsqrt(degree)
    powers = 2 ** jnp.arange(VECTORS, dtype=jnp.int32)
    vectors = (start_bits[None, :] // powers[:, None] % 2).astype(jnp.float32).reshape(VECTORS, NBLOCKS, BLOCK)
    highest = lax.Precision.HIGHEST
    for iteration in range(ITERS):
        projection = jnp.einsum('kbi,bi->k', vectors, root_degree, precision=highest)
        scaled = vectors * inverse
        neighbours = jnp.concatenate([jnp.roll(scaled, 1, axis=1), scaled, jnp.roll(scaled, -1, axis=1)], axis=2)
        applied = jnp.einsum('bic,kbc->kbi', affinity, neighbours, precision=highest)
        deflated = applied * inverse - root_degree * (projection / degree_total)[:, None, None]
        gram_matrix = jnp.einsum('kbi,mbi->km', deflated, deflated, precision=highest) / EVENTS
        factor = jnp.linalg.cholesky(gram_matrix)
        solved = lax.linalg.triangular_solve(factor, deflated.reshape(VECTORS, EVENTS), left_side=True, lower=True)
        vectors = solved.reshape(VECTORS, NBLOCKS, BLOCK)
    return vectors.reshape(VECTORS, EVENTS)
```

```python
import functools

import jax
import jax.numpy as jnp
from jax import lax
from jax.experimental import pallas as pl
from jax.experimental.pallas import tpu as pltpu
from jax.sharding import PartitionSpec as P

SAMPLES = 1024
MAXLAG = 64
LAGS = 65
OFFBITS = 6
VECTORS = 16
ITERS = 3
COMPS = 3
GROUP = 5
PADDED = SAMPLES + 2 * MAXLAG
SHARPNESS = 64.0
MESH = pl.DeviceIdType.MESH
HIGHEST = lax.Precision.HIGHEST


def kernel(
    nblk,
    nlag,
    own,
    events,
    x_ref,
    shift_ref,
    bits_ref,
    out_ref,
    wall,
    wprev,
    pad,
    shifted,
    columns,
    aff,
    beyond,
    bitbuf,
    dg,
    yn,
    gm,
    wave_send,
    wave_recv,
    bit_send,
    bit_recv,
    aff_send,
    aff_recv,
    far_send,
    far_recv,
    dg_send,
    dg_recv,
    yn_send,
    yn_recv,
    gm_send,
    gm_recv,
):
    b = lax.axis_index("blk")
    me = lax.axis_index("lag")
    width = nlag * own

    def block_at(step):
        return lax.rem(b + step + nblk, nblk)

    def member_at(step):
        return lax.rem(me + step, nlag)

    def remote(src, dst, send, recv, blk, lag):
        return pltpu.make_async_remote_copy(
            src_ref=src,
            dst_ref=dst,
            send_sem=send,
            recv_sem=recv,
            device_id=(blk, lag),
            device_id_type=MESH,
        )

    barrier = pltpu.get_barrier_semaphore()
    partners = [(0, k) for k in range(1, nlag)]
    partners += [(s, k) for s in (1, -1) for k in range(nlag)]
    partners += [(s, 0) for s in range(2, nblk - 1)]
    for step, k in partners:
        pl.semaphore_signal(
            barrier, inc=1, device_id=(block_at(step), member_at(k)), device_id_type=MESH
        )

    x = x_ref[...]
    shift = jnp.broadcast_to(shift_ref[...], x.shape)
    for k in range(OFFBITS):
        moved = pltpu.roll(x, SAMPLES - 2**k, 1)
        x = jnp.where((lax.shift_right_logical(shift, k) & 1) == 1, moved, x)
    lane = lax.broadcasted_iota(jnp.int32, x.shape, 1)
    x = jnp.where(lane + shift < SAMPLES, x, 0.0)
    squares = jnp.sum(x * x, axis=1, keepdims=True)
    energy = squares[0:own] + squares[own : 2 * own] + squares[2 * own : 3 * own]
    scale = lax.rsqrt(energy + 1e-06)
    for c in range(COMPS):
        unit = (x[c * own : (c + 1) * own] * scale).astype(jnp.bfloat16)
        wall[me, :, c * SAMPLES : (c + 1) * SAMPLES] = unit
    bitbuf[0] = bits_ref[...]

    pl.semaphore_wait(barrier, len(partners))

    wave_copies = []
    for k in range(1, nlag):
        wave_copies.append(
            remote(wall.at[me], wall.at[me], wave_send.at[k], wave_recv.at[k], b, member_at(k))
        )
    wave_copies.append(
        remote(wall.at[me], wprev, wave_send.at[0], wave_recv.at[0], block_at(1), me)
    )
    bit_copies = [
        remote(bitbuf.at[0], bitbuf.at[k], bit_send.at[k], bit_recv.at[k], b, member_at(k))
        for k in range(1, nlag)
    ]
    for copy in wave_copies + bit_copies:
        copy.start()

    def place(rows, first):
        for c in range(COMPS):
            piece = rows[:, c * SAMPLES : (c + 1) * SAMPLES].astype(jnp.float32)
            wide = jnp.concatenate([piece, jnp.zeros((own, 2 * MAXLAG), jnp.float32)], 1)
            pad[first : first + own, c * PADDED : (c + 1) * PADDED] = pltpu.roll(
                wide, MAXLAG, 1
            ).astype(pad.dtype)

    place(wall[me], 0)
    for copy in wave_copies:
        copy.wait()
    place(wprev[...], own)
    columns[...] = wall[...].reshape(width, COMPS * SAMPLES).T

    rows = 2 * own

    def one_group(index, running):
        for c in range(COMPS):
            wide = pad[:, c * PADDED : (c + 1) * PADDED]
            for o in range(GROUP):
                moved = wide if o == 0 else pltpu.roll(wide, PADDED - 2 * o, 1)
                shifted[o * rows : (o + 1) * rows, c * SAMPLES : (c + 1) * SAMPLES] = moved[
                    :, :SAMPLES
                ].astype(jnp.bfloat16)
            pad[:, c * PADDED : (c + 1) * PADDED] = pltpu.roll(wide, PADDED - 2 * GROUP, 1)
        scores = jnp.dot(shifted[...], columns[...], preferred_element_type=jnp.float32)
        weights = jnp.exp(SHARPNESS * scores)
        for o in range(GROUP):
            running = running + weights[o * rows : (o + 1) * rows]
        return running

    running = lax.fori_loop(
        0, LAGS // GROUP, one_group, jnp.zeros((rows, width), jnp.float32)
    )
    row_id = lax.broadcasted_iota(jnp.int32, (own, width), 0)
    lane_id = lax.broadcasted_iota(jnp.int32, (own, width), 1)
    aff[me, 1] = jnp.where(lane_id == row_id + me * own, 0.0, running[0:own])
    aff[me, 0] = running[own : 2 * own]

    far_copies = [
        remote(
            aff.at[me, 0], beyond.at[me], far_send.at[k], far_recv.at[k], block_at(-1), member_at(k)
        )
        for k in range(nlag)
    ]
    aff_copies = [
        remote(aff.at[me], aff.at[me], aff_send.at[k], aff_recv.at[k], b, member_at(k))
        for k in range(1, nlag)
    ]
    for copy in far_copies + aff_copies:
        copy.start()
    for copy in bit_copies + far_copies + aff_copies:
        copy.wait()

    before = aff[:, 0].reshape(width, width)
    centre = aff[:, 1].reshape(width, width)
    after = beyond[...].reshape(width, width).T
    degree = jnp.sum(before + centre + after, axis=0, keepdims=True)
    code = bitbuf[0]
    for k in range(1, nlag):
        code = code + bitbuf[k]
    first_row = lax.broadcasted_iota(jnp.int32, (8, width), 0) == 0
    dg[0] = jnp.where(first_row, jnp.broadcast_to(degree, (8, width)), code)
    dg_copies = [
        remote(dg.at[0], dg.at[s], dg_send.at[s], dg_recv.at[s], block_at(s), me)
        for s in range(1, nblk)
    ]
    for copy in dg_copies:
        copy.start()
    for copy in dg_copies:
        copy.wait()

    powers = lax.broadcasted_iota(jnp.int32, (VECTORS, width), 0)
    total_row = jnp.zeros((1, width), jnp.float32)
    proj_lanes = jnp.zeros((VECTORS, width), jnp.float32)
    near = {}
    for s in range(nblk):
        tile = dg[s]
        deg = tile[0:1]
        bits = jnp.broadcast_to(tile[1:2].astype(jnp.int32), (VECTORS, width))
        start = (lax.shift_right_logical(bits, powers) & 1).astype(jnp.float32)
        total_row = total_row + deg
        proj_lanes = proj_lanes + start * jnp.sqrt(deg)
        if s in (0, 1, nblk - 1):
            near[s] = (start, lax.rsqrt(deg), jnp.sqrt(deg))
    total = jnp.sum(total_row, axis=1, keepdims=True)
    projection = jnp.sum(proj_lanes, axis=1, keepdims=True)
    order = (1, 0, nblk - 1)
    inverses = [near[s][1] for s in order]
    vectors = [near[s][0] for s in order]
    inverse, root = near[0][1], near[0][2]
    sub = lax.broadcasted_iota(jnp.int32, (VECTORS, width), 0)
    lane = lax.broadcasted_iota(jnp.int32, (VECTORS, width), 1)

    for it in range(ITERS):
        last = it == ITERS - 1
        applied = jnp.zeros((VECTORS, width), jnp.float32)
        for vector, inv, part in zip(vectors, inverses, (before, centre, after)):
            applied = applied + jnp.dot(
                vector * inv, part, precision=HIGHEST, preferred_element_type=jnp.float32
            )
        deflated = applied * inverse - root * (projection / total)
        yn[it, 0] = deflated
        copies = []
        if not last:
            copies = [
                remote(
                    yn.at[it, 0],
                    yn.at[it, slot],
                    yn_send.at[it, slot],
                    yn_recv.at[it, slot],
                    block_at(step),
                    me,
                )
                for slot, step in ((1, 1), (2, -1))
            ]
            for copy in copies:
                copy.start()
        gram = lax.dot_general(
            deflated,
            deflated,
            (((1,), (1,)), ((), ())),
            precision=HIGHEST,
            preferred_element_type=jnp.float32,
        )
        carried = jnp.sum(deflated * root, axis=1, keepdims=True)
        wide = jnp.concatenate([gram, jnp.zeros((VECTORS, width - VECTORS), jnp.float32)], 1)
        gm[it, 0] = jnp.where(lane == VECTORS, carried, wide)
        gm_copies = [
            remote(
                gm.at[it, 0],
                gm.at[it, s],
                gm_send.at[it, s],
                gm_recv.at[it, s],
                block_at(s),
                me,
            )
            for s in range(1, nblk)
        ]
        for copy in gm_copies:
            copy.start()
        for copy in gm_copies + copies:
            copy.wait()
        table = gm[it, 0]
        for s in range(1, nblk):
            table = table + gm[it, s]
        table = jnp.where(lane < VECTORS, table / events, table)
        tiles = [table, deflated] if last else [table, yn[it, 1], deflated, yn[it, 2]]
        for k in range(VECTORS):
            column = tiles[0][:, k : k + 1]
            r = lax.rsqrt(tiles[0][k : k + 1, k : k + 1])
            factor = jnp.where(sub[:, 0:1] > k, column * r, 0.0)
            updated = []
            for tile in tiles:
                pivot = tile[k : k + 1] * r
                updated.append(jnp.where(sub == k, pivot, tile - factor * pivot))
            tiles = updated
        projection = tiles[0][:, VECTORS : VECTORS + 1]
        vectors = tiles[1:]

    result = jnp.zeros((VECTORS, own), jnp.float32)
    for k in range(nlag):
        result = jnp.where(me == k, vectors[0][:, k * own : (k + 1) * own], result)
    out_ref[...] = result


def local(nblk, nlag, seismograms, onset_shift, start_bits):
    own = seismograms.shape[0]
    width = nlag * own
    events = own * nblk * nlag
    me = lax.axis_index("lag")
    records = jnp.transpose(seismograms, (1, 0, 2)).reshape(COMPS * own, SAMPLES)
    shift = jnp.tile(onset_shift, COMPS)[:, None]
    places = jnp.arange(width, dtype=jnp.int32) // own
    codes = jnp.where(places == me, jnp.tile(start_bits, nlag), 0).astype(jnp.float32)
    codes = jnp.broadcast_to(codes[None, :], (8, width))
    f32, bf16 = jnp.float32, jnp.bfloat16
    dma = pltpu.SemaphoreType.DMA
    flat = COMPS * SAMPLES
    return pl.pallas_call(
        functools.partial(kernel, nblk, nlag, own, events),
        out_shape=jax.ShapeDtypeStruct((VECTORS, own), f32),
        in_specs=[pl.BlockSpec(memory_space=pltpu.VMEM)] * 3,
        out_specs=pl.BlockSpec(memory_space=pltpu.VMEM),
        scratch_shapes=[
            pltpu.VMEM((nlag, own, flat), bf16),
            pltpu.VMEM((own, flat), bf16),
            pltpu.VMEM((2 * own, COMPS * PADDED), PAD_DTYPE),
            pltpu.VMEM((GROUP * 2 * own, flat), bf16),
            pltpu.VMEM((flat, width), bf16),
            pltpu.VMEM((nlag, 2, own, width), f32),
            pltpu.VMEM((nlag, own, width), f32),
            pltpu.VMEM((nlag, 8, width), f32),
            pltpu.VMEM((nblk, 8, width), f32),
            pltpu.VMEM((ITERS, 3, VECTORS, width), f32),
            pltpu.VMEM((ITERS, nblk, VECTORS, width), f32),
            dma((nlag,)),
            dma((nlag,)),
            dma((nlag,)),
            dma((nlag,)),
            dma((nlag,)),
            dma((nlag,)),
            dma((nlag,)),
            dma((nlag,)),
            dma((nblk,)),
            dma((nblk,)),
            dma((ITERS, 3)),
            dma((ITERS, 3)),
            dma((ITERS, nblk)),
            dma((ITERS, nblk)),
        ],
        compiler_params=pltpu.CompilerParams(
            collective_id=0, has_side_effects=True, vmem_limit_bytes=40 * 1024 * 1024
        ),
    )(records, shift, codes)


PAD_DTYPE = jnp.float32


def solution(mesh):
    spec = P(("blk", "lag"))
    return jax.shard_map(
        functools.partial(local, mesh.shape["blk"], mesh.shape["lag"]),
        mesh=mesh,
        in_specs=(P(("blk", "lag"), None, None), spec, spec),
        out_specs=P(None, ("blk", "lag")),
        check_vma=False,
    )
```

```python
import functools

import jax
import jax.numpy as jnp
from jax import lax
from jax.experimental import pallas as pl
from jax.experimental.pallas import tpu as pltpu
from jax.sharding import PartitionSpec as P

SAMPLES = 1024
MAXLAG = 64
LAGS = 65
OFFBITS = 6
VECTORS = 16
ITERS = 3
COMPS = 3
GROUP = 13
PADDED = SAMPLES + 2 * MAXLAG
SHARPNESS = 64.0
MESH = pl.DeviceIdType.MESH
HIGHEST = lax.Precision.HIGHEST


def kernel(
    nblk,
    nlag,
    own,
    events,
    x_hbm,
    shift_hbm,
    bits_hbm,
    out_ref,
    x_ref,
    shift_ref,
    bits_ref,
    wall,
    wprev,
    pad,
    shifted_own,
    shifted_before,
    columns,
    aff,
    beyond,
    bitbuf,
    dg,
    yn,
    gm,
    load_sem,
    wave_send,
    wave_recv,
    bit_send,
    bit_recv,
    aff_send,
    aff_recv,
    far_send,
    far_recv,
    dg_send,
    dg_recv,
    yn_send,
    yn_recv,
    gm_send,
    gm_recv,
):
    b = lax.axis_index("blk")
    me = lax.axis_index("lag")
    width = nlag * own

    def block_at(step):
        return lax.rem(b + step + nblk, nblk)

    def member_at(step):
        return lax.rem(me + step, nlag)

    def remote(src, dst, send, recv, blk, lag):
        return pltpu.make_async_remote_copy(
            src_ref=src,
            dst_ref=dst,
            send_sem=send,
            recv_sem=recv,
            device_id=(blk, lag),
            device_id_type=MESH,
        )

    loads = [
        pltpu.make_async_copy(source, target, load_sem.at[k])
        for k, (source, target) in enumerate(
            ((shift_hbm, shift_ref), (bits_hbm, bits_ref), (x_hbm, x_ref))
        )
    ]
    for load in loads:
        load.start()
    barrier = pltpu.get_barrier_semaphore()
    partners = [(0, k) for k in range(1, nlag)]
    partners += [(s, k) for s in (1, -1) for k in range(nlag)]
    partners += [(s, 0) for s in range(2, nblk - 1)]
    for step, k in partners:
        pl.semaphore_signal(
            barrier, inc=1, device_id=(block_at(step), member_at(k)), device_id_type=MESH
        )

    for load in loads:
        load.wait()
    x = x_ref[...]
    diagonal = lax.broadcasted_iota(jnp.int32, (own, own), 0) == lax.broadcasted_iota(
        jnp.int32, (own, own), 1
    )
    spread = jnp.broadcast_to(shift_ref[...].astype(jnp.float32), (own, own))
    column = jnp.sum(jnp.where(diagonal, spread, 0.0), axis=1, keepdims=True).astype(jnp.int32)
    shift = jnp.concatenate([jnp.broadcast_to(column, (own, SAMPLES))] * COMPS, 0)
    for k in range(OFFBITS):
        moved = pltpu.roll(x, SAMPLES - 2**k, 1)
        x = jnp.where((lax.shift_right_logical(shift, k) & 1) == 1, moved, x)
    lane = lax.broadcasted_iota(jnp.int32, x.shape, 1)
    x = jnp.where(lane + shift < SAMPLES, x, 0.0)
    squares = jnp.sum(x * x, axis=1, keepdims=True)
    energy = squares[0:own] + squares[own : 2 * own] + squares[2 * own : 3 * own]
    scale = lax.rsqrt(energy + 1e-06)
    for c in range(COMPS):
        unit = (x[c * own : (c + 1) * own] * scale).astype(jnp.bfloat16)
        wall[me, :, c * SAMPLES : (c + 1) * SAMPLES] = unit
    codes = jnp.concatenate([bits_ref[...].astype(jnp.float32)] * nlag, 1)
    place_id = lax.broadcasted_iota(jnp.int32, (8, width), 1)
    mine = (place_id >= me * own) & (place_id < (me + 1) * own)
    bitbuf[0] = jnp.where(mine, jnp.broadcast_to(codes, (8, width)), 0.0)

    pl.semaphore_wait(barrier, len(partners))

    sibling = me + 1 - 2 * lax.rem(me, 2)
    across = member_at(2)
    half = own // 2
    to_next = remote(wall.at[me], wprev, wave_send.at[0], wave_recv.at[0], block_at(1), me)
    to_sibling = remote(wall.at[me], wall.at[me], wave_send.at[1], wave_recv.at[1], b, sibling)

    def halves(slot, first_sem, member):
        return [
            remote(
                wall.at[slot, h * half : (h + 1) * half],
                wall.at[slot, h * half : (h + 1) * half],
                wave_send.at[first_sem + h],
                wave_recv.at[first_sem + h],
                b,
                member,
            )
            for h in range(2)
        ]

    to_across = halves(me, 2, across)
    relayed = halves(across, 4, sibling)
    wave_copies = to_across + [to_next, to_sibling]
    bit_copies = [
        remote(bitbuf.at[0], bitbuf.at[k], bit_send.at[k], bit_recv.at[k], b, member_at(k))
        for k in range(1, nlag)
    ]
    for copy in wave_copies + bit_copies:
        copy.start()

    def place(rows):
        for c in range(COMPS):
            piece = rows[:, c * SAMPLES : (c + 1) * SAMPLES].astype(jnp.float32)
            wide = jnp.concatenate([piece, jnp.zeros((own, 2 * MAXLAG), jnp.float32)], 1)
            pad[:, c * PADDED : (c + 1) * PADDED] = pltpu.roll(wide, MAXLAG, 1).astype(pad.dtype)

    taken = GROUP * own

    def slide(index, target):
        for c in range(COMPS):
            wide = pad[:, c * PADDED : (c + 1) * PADDED]
            for o in range(GROUP):
                moved = wide if o == 0 else pltpu.roll(wide, PADDED - 2 * o, 1)
                rows = pl.ds(pl.multiple_of(index * taken + o * own, own), own)
                target[rows, c * SAMPLES : (c + 1) * SAMPLES] = moved[:, :SAMPLES].astype(
                    jnp.bfloat16
                )
            pad[:, c * PADDED : (c + 1) * PADDED] = pltpu.roll(wide, PADDED - 2 * GROUP, 1)

    def weigh(index, source, running):
        rows = pl.ds(pl.multiple_of(index * taken, taken), taken)
        scores = jnp.dot(source[rows, :], columns[...], preferred_element_type=jnp.float32)
        weights = jnp.exp(SHARPNESS * scores)
        for o in range(GROUP):
            running = running + weights[o * own : (o + 1) * own]
        return running

    place(wall[me])

    def slide_own(index, carry):
        slide(index, shifted_own)
        return carry

    groups = LAGS // GROUP
    lax.fori_loop(0, groups, slide_own, 0)
    for arriving, passing in zip(to_across, relayed):
        arriving.wait_recv()
        passing.start()
    to_next.wait()
    place(wprev[...])
    to_sibling.wait()
    for arriving, passing in zip(to_across, relayed):
        arriving.wait_send()
        passing.wait()
    columns[...] = wall[...].reshape(width, COMPS * SAMPLES).T

    def both(index, running):
        slide(index, shifted_before)
        return weigh(index, shifted_own, running)

    zeros = jnp.zeros((own, width), jnp.float32)
    running = lax.fori_loop(0, groups, both, zeros)
    row_id = lax.broadcasted_iota(jnp.int32, (own, width), 0)
    lane_id = lax.broadcasted_iota(jnp.int32, (own, width), 1)
    aff[1, me] = jnp.where(lane_id == row_id + me * own, 0.0, running)

    def pieces(part):
        return [
            remote(
                aff.at[part, me],
                aff.at[part, me],
                aff_send.at[part, k],
                aff_recv.at[part, k],
                b,
                member_at(k),
            )
            for k in range(1, nlag)
        ]

    centre_copies = pieces(1)
    for copy in centre_copies:
        copy.start()

    def only(index, running):
        return weigh(index, shifted_before, running)

    aff[0, me] = lax.fori_loop(0, groups, only, zeros)
    far_copies = [
        remote(
            aff.at[0, me], beyond.at[me], far_send.at[k], far_recv.at[k], block_at(-1), member_at(k)
        )
        for k in range(nlag)
    ]
    before_copies = pieces(0)
    for copy in far_copies + before_copies:
        copy.start()
    for copy in bit_copies + centre_copies + before_copies + far_copies:
        copy.wait()

    before = aff[0].reshape(width, width)
    centre = aff[1].reshape(width, width)
    after = beyond[...].reshape(width, width).T
    degree = jnp.sum(before + centre + after, axis=0, keepdims=True)
    code = bitbuf[0]
    for k in range(1, nlag):
        code = code + bitbuf[k]
    first_row = lax.broadcasted_iota(jnp.int32, (8, width), 0) == 0
    dg[0] = jnp.where(first_row, jnp.broadcast_to(degree, (8, width)), code)
    dg_copies = [
        remote(dg.at[0], dg.at[s], dg_send.at[s], dg_recv.at[s], block_at(s), me)
        for s in range(1, nblk)
    ]
    for copy in dg_copies:
        copy.start()
    for copy in dg_copies:
        copy.wait()

    powers = lax.broadcasted_iota(jnp.int32, (VECTORS, width), 0)
    total_row = jnp.zeros((1, width), jnp.float32)
    proj_lanes = jnp.zeros((VECTORS, width), jnp.float32)
    near = {}
    for s in range(nblk):
        tile = dg[s]
        deg = tile[0:1]
        bits = jnp.broadcast_to(tile[1:2].astype(jnp.int32), (VECTORS, width))
        start = (lax.shift_right_logical(bits, powers) & 1).astype(jnp.float32)
        total_row = total_row + deg
        proj_lanes = proj_lanes + start * jnp.sqrt(deg)
        if s in (0, 1, nblk - 1):
            near[s] = (start, lax.rsqrt(deg), jnp.sqrt(deg))
    total = jnp.sum(total_row, axis=1, keepdims=True)
    projection = jnp.sum(proj_lanes, axis=1, keepdims=True)
    order = (1, 0, nblk - 1)
    inverses = [near[s][1] for s in order]
    vectors = [near[s][0] for s in order]
    inverse, root = near[0][1], near[0][2]
    sub = lax.broadcasted_iota(jnp.int32, (VECTORS, width), 0)
    lane = lax.broadcasted_iota(jnp.int32, (VECTORS, width), 1)

    for it in range(ITERS):
        last = it == ITERS - 1
        applied = jnp.zeros((VECTORS, width), jnp.float32)
        for vector, inv, part in zip(vectors, inverses, (before, centre, after)):
            applied = applied + jnp.dot(
                vector * inv, part, precision=HIGHEST, preferred_element_type=jnp.float32
            )
        deflated = applied * inverse - root * (projection / total)
        yn[it, 0] = deflated
        copies = []
        if not last:
            copies = [
                remote(
                    yn.at[it, 0],
                    yn.at[it, slot],
                    yn_send.at[it, slot],
                    yn_recv.at[it, slot],
                    block_at(step),
                    me,
                )
                for slot, step in ((1, 1), (2, -1))
            ]
            for copy in copies:
                copy.start()
        gram = lax.dot_general(
            deflated,
            deflated,
            (((1,), (1,)), ((), ())),
            precision=HIGHEST,
            preferred_element_type=jnp.float32,
        )
        carried = jnp.sum(deflated * root, axis=1, keepdims=True)
        wide = jnp.concatenate([gram, jnp.zeros((VECTORS, width - VECTORS), jnp.float32)], 1)
        gm[it, 0] = jnp.where(lane == VECTORS, carried, wide)
        gm_copies = [
            remote(
                gm.at[it, 0],
                gm.at[it, s],
                gm_send.at[it, s],
                gm_recv.at[it, s],
                block_at(s),
                me,
            )
            for s in range(1, nblk)
        ]
        for copy in gm_copies:
            copy.start()
        for copy in gm_copies + copies:
            copy.wait()
        table = gm[it, 0]
        for s in range(1, nblk):
            table = table + gm[it, s]
        table = jnp.where(lane < VECTORS, table / events, table)
        tiles = [table, deflated] if last else [table, yn[it, 1], deflated, yn[it, 2]]
        for k in range(VECTORS):
            column = tiles[0][:, k : k + 1]
            r = lax.rsqrt(tiles[0][k : k + 1, k : k + 1])
            factor = jnp.where(sub[:, 0:1] > k, column * r, 0.0)
            updated = []
            for tile in tiles:
                pivot = tile[k : k + 1] * r
                updated.append(jnp.where(sub == k, pivot, tile - factor * pivot))
            tiles = updated
        projection = tiles[0][:, VECTORS : VECTORS + 1]
        vectors = tiles[1:]

    result = jnp.zeros((VECTORS, own), jnp.float32)
    for k in range(nlag):
        result = jnp.where(me == k, vectors[0][:, k * own : (k + 1) * own], result)
    out_ref[...] = result


def local(nblk, nlag, seismograms, onset_shift, start_bits):
    own = seismograms.shape[0]
    width = nlag * own
    events = own * nblk * nlag
    records = jnp.transpose(seismograms, (1, 0, 2)).reshape(COMPS * own, SAMPLES)
    f32, bf16 = jnp.float32, jnp.bfloat16
    dma = pltpu.SemaphoreType.DMA
    flat = COMPS * SAMPLES
    return pl.pallas_call(
        functools.partial(kernel, nblk, nlag, own, events),
        out_shape=jax.ShapeDtypeStruct((VECTORS, own), f32),
        in_specs=[pl.BlockSpec(memory_space=pltpu.HBM)] * 3,
        out_specs=pl.BlockSpec(memory_space=pltpu.VMEM),
        scratch_shapes=[
            pltpu.VMEM((COMPS * own, SAMPLES), f32),
            pltpu.VMEM((1, own), jnp.int32),
            pltpu.VMEM((1, own), jnp.int32),
            pltpu.VMEM((nlag, own, flat), bf16),
            pltpu.VMEM((own, flat), bf16),
            pltpu.VMEM((own, COMPS * PADDED), PAD_DTYPE),
            pltpu.VMEM((LAGS * own, flat), bf16),
            pltpu.VMEM((LAGS * own, flat), bf16),
            pltpu.VMEM((flat, width), bf16),
            pltpu.VMEM((2, nlag, own, width), f32),
            pltpu.VMEM((nlag, own, width), f32),
            pltpu.VMEM((nlag, 8, width), f32),
            pltpu.VMEM((nblk, 8, width), f32),
            pltpu.VMEM((ITERS, 3, VECTORS, width), f32),
            pltpu.VMEM((ITERS, nblk, VECTORS, width), f32),
            dma((3,)),
            dma((6,)),
            dma((6,)),
            dma((nlag,)),
            dma((nlag,)),
            dma((2, nlag)),
            dma((2, nlag)),
            dma((nlag,)),
            dma((nlag,)),
            dma((nblk,)),
            dma((nblk,)),
            dma((ITERS, 3)),
            dma((ITERS, 3)),
            dma((ITERS, nblk)),
            dma((ITERS, nblk)),
        ],
        compiler_params=pltpu.CompilerParams(
            collective_id=0, has_side_effects=True, vmem_limit_bytes=50 * 1024 * 1024
        ),
    )(records, onset_shift[None, :], start_bits[None, :])


PAD_DTYPE = jnp.float32


def solution(mesh):
    spec = P(("blk", "lag"))
    return jax.shard_map(
        functools.partial(local, mesh.shape["blk"], mesh.shape["lag"]),
        mesh=mesh,
        in_specs=(P(("blk", "lag"), None, None), spec, spec),
        out_specs=P(None, ("blk", "lag")),
        check_vma=False,
    )
```

```python
import functools

import jax
import jax.numpy as jnp
from jax import lax
from jax.experimental import pallas as pl
from jax.experimental.pallas import tpu as pltpu
from jax.sharding import PartitionSpec as P

SAMPLES = 1024
MAXLAG = 64
LAGS = 65
OFFBITS = 6
VECTORS = 16
ITERS = 3
COMPS = 3
GROUP = 13
PADDED = SAMPLES + 2 * MAXLAG
SHARPNESS = 64.0
MESH = pl.DeviceIdType.MESH
HIGHEST = lax.Precision.HIGHEST


def kernel(
    nblk,
    nlag,
    own,
    events,
    x_hbm,
    shift_hbm,
    bits_hbm,
    out_ref,
    x_ref,
    shift_ref,
    bits_ref,
    wall,
    wprev,
    pad,
    shifted_own,
    shifted_before,
    columns,
    aff,
    beyond,
    parts,
    dg,
    yn,
    gm,
    load_sem,
    wave_send,
    wave_recv,
    part_send,
    part_recv,
    aff_send,
    aff_recv,
    far_send,
    far_recv,
    dg_send,
    dg_recv,
    yn_send,
    yn_recv,
    gm_send,
    gm_recv,
):
    b = lax.axis_index("blk")
    me = lax.axis_index("lag")
    width = nlag * own

    def block_at(step):
        return lax.rem(b + step + nblk, nblk)

    def member_at(step):
        return lax.rem(me + step, nlag)

    def remote(src, dst, send, recv, blk, lag):
        return pltpu.make_async_remote_copy(
            src_ref=src,
            dst_ref=dst,
            send_sem=send,
            recv_sem=recv,
            device_id=(blk, lag),
            device_id_type=MESH,
        )

    loads = [
        pltpu.make_async_copy(source, target, load_sem.at[k])
        for k, (source, target) in enumerate(
            ((shift_hbm, shift_ref), (bits_hbm, bits_ref), (x_hbm, x_ref))
        )
    ]
    for load in loads:
        load.start()
    barrier = pltpu.get_barrier_semaphore()
    partners = [(0, k) for k in range(1, nlag)]
    partners += [(s, k) for s in (1, -1) for k in range(nlag)]
    partners += [(s, 0) for s in range(2, nblk - 1)]
    for step, k in partners:
        pl.semaphore_signal(
            barrier, inc=1, device_id=(block_at(step), member_at(k)), device_id_type=MESH
        )

    for load in loads:
        load.wait()
    x = x_ref[...]
    diagonal = lax.broadcasted_iota(jnp.int32, (own, own), 0) == lax.broadcasted_iota(
        jnp.int32, (own, own), 1
    )
    spread = jnp.broadcast_to(shift_ref[...].astype(jnp.float32), (own, own))
    column = jnp.sum(jnp.where(diagonal, spread, 0.0), axis=1, keepdims=True).astype(jnp.int32)
    shift = jnp.concatenate([jnp.broadcast_to(column, (own, SAMPLES))] * COMPS, 0)
    for k in range(OFFBITS):
        moved = pltpu.roll(x, SAMPLES - 2**k, 1)
        x = jnp.where((lax.shift_right_logical(shift, k) & 1) == 1, moved, x)
    lane = lax.broadcasted_iota(jnp.int32, x.shape, 1)
    x = jnp.where(lane + shift < SAMPLES, x, 0.0)
    squares = jnp.sum(x * x, axis=1, keepdims=True)
    energy = squares[0:own] + squares[own : 2 * own] + squares[2 * own : 3 * own]
    scale = lax.rsqrt(energy + 1e-06)
    for c in range(COMPS):
        unit = (x[c * own : (c + 1) * own] * scale).astype(jnp.bfloat16)
        wall[me, :, c * SAMPLES : (c + 1) * SAMPLES] = unit
    codes = jnp.concatenate([bits_ref[...].astype(jnp.float32)] * nlag, 1)
    place_id = lax.broadcasted_iota(jnp.int32, (8, width), 1)
    mine = (place_id >= me * own) & (place_id < (me + 1) * own)
    codes = jnp.where(mine[0:1], codes, 0.0)

    pl.semaphore_wait(barrier, len(partners))

    sibling = me + 1 - 2 * lax.rem(me, 2)
    across = member_at(2)
    half = own // 2
    to_next = remote(wall.at[me], wprev, wave_send.at[0], wave_recv.at[0], block_at(1), me)
    to_sibling = remote(wall.at[me], wall.at[me], wave_send.at[1], wave_recv.at[1], b, sibling)

    def halves(slot, first_sem, member):
        return [
            remote(
                wall.at[slot, h * half : (h + 1) * half],
                wall.at[slot, h * half : (h + 1) * half],
                wave_send.at[first_sem + h],
                wave_recv.at[first_sem + h],
                b,
                member,
            )
            for h in range(2)
        ]

    to_across = halves(me, 2, across)
    relayed = halves(across, 4, sibling)
    wave_copies = to_across + [to_next, to_sibling]
    for copy in wave_copies:
        copy.start()

    def place(rows):
        for c in range(COMPS):
            piece = rows[:, c * SAMPLES : (c + 1) * SAMPLES].astype(jnp.float32)
            wide = jnp.concatenate([piece, jnp.zeros((own, 2 * MAXLAG), jnp.float32)], 1)
            pad[:, c * PADDED : (c + 1) * PADDED] = pltpu.roll(wide, MAXLAG, 1).astype(pad.dtype)

    taken = GROUP * own

    def at(first, size):
        return pl.ds(first if isinstance(first, int) else pl.multiple_of(first, size), size)

    def slide(index, target):
        for c in range(COMPS):
            wide = pad[:, c * PADDED : (c + 1) * PADDED]
            for o in range(GROUP):
                moved = wide if o == 0 else pltpu.roll(wide, PADDED - 2 * o, 1)
                rows = at(index * taken + o * own, own)
                target[rows, c * SAMPLES : (c + 1) * SAMPLES] = moved[:, :SAMPLES].astype(
                    jnp.bfloat16
                )
            pad[:, c * PADDED : (c + 1) * PADDED] = pltpu.roll(wide, PADDED - 2 * GROUP, 1)

    def weigh(index, source, running):
        rows = at(index * taken, taken)
        scores = jnp.dot(source[rows, :], columns[...], preferred_element_type=jnp.float32)
        weights = jnp.exp(SHARPNESS * scores)
        for o in range(GROUP):
            running = running + weights[o * own : (o + 1) * own]
        return running

    place(wall[me])

    def slide_own(index, carry):
        slide(index, shifted_own)
        return carry

    groups = LAGS // GROUP
    lax.fori_loop(0, groups, slide_own, 0)
    for arriving, passing in zip(to_across, relayed):
        arriving.wait_recv()
        passing.start()
    to_next.wait()
    place(wprev[...])
    to_sibling.wait()
    for arriving, passing in zip(to_across, relayed):
        arriving.wait_send()
        passing.wait()
    columns[...] = wall[...].reshape(width, COMPS * SAMPLES).T

    def both(index, running):
        slide(index, shifted_before)
        return weigh(index, shifted_own, running)

    zeros = jnp.zeros((own, width), jnp.float32)
    running = lax.fori_loop(0, groups, both, zeros)
    row_id = lax.broadcasted_iota(jnp.int32, (own, width), 0)
    lane_id = lax.broadcasted_iota(jnp.int32, (own, width), 1)
    aff[1, me] = jnp.where(lane_id == row_id + me * own, 0.0, running)

    def pieces(part):
        return [
            remote(
                aff.at[part, me],
                aff.at[part, me],
                aff_send.at[part, k],
                aff_recv.at[part, k],
                b,
                member_at(k),
            )
            for k in range(1, nlag)
        ]

    centre_copies = pieces(1)
    for copy in centre_copies:
        copy.start()

    def only(index, running):
        return weigh(index, shifted_before, running)

    running = lax.fori_loop(0, groups, only, zeros)
    aff[0, me] = running
    far_copies = [
        remote(
            aff.at[0, me], beyond.at[me], far_send.at[k], far_recv.at[k], block_at(-1), member_at(k)
        )
        for k in range(nlag)
    ]
    before_copies = pieces(0)
    for copy in far_copies + before_copies:
        copy.start()

    direct = jnp.sum(aff[1, me] + running, axis=0, keepdims=True)
    totals = jnp.broadcast_to(jnp.sum(running, axis=1, keepdims=True), (own, own))
    turned = jnp.sum(jnp.where(diagonal, totals, 0.0), axis=0, keepdims=True)
    turned = jnp.where(mine[0:1], jnp.concatenate([turned] * nlag, 1), 0.0)
    sub_id = lax.broadcasted_iota(jnp.int32, (8, width), 0)
    dg[0] = jnp.where(sub_id == 0, direct, jnp.where(sub_id == 1, turned, codes))
    dg_copies = [
        remote(dg.at[0], dg.at[s], dg_send.at[s], dg_recv.at[s], block_at(s), me)
        for s in range(1, nblk)
    ]
    for copy in dg_copies:
        copy.start()
    for copy in dg_copies:
        copy.wait()
    for s in range(nblk):
        parts[0, s : s + 1] = dg[s, 0:1] + dg[(s - 1) % nblk, 1:2]
        parts[0, nblk + s : nblk + s + 1] = dg[s, 2:3]
    part_copies = [
        remote(parts.at[0], parts.at[k], part_send.at[k], part_recv.at[k], b, member_at(k))
        for k in range(1, nlag)
    ]
    for copy in part_copies:
        copy.start()
    for copy in centre_copies + before_copies + far_copies + part_copies:
        copy.wait()

    before = aff[0].reshape(width, width)
    centre = aff[1].reshape(width, width)
    after = beyond[...].reshape(width, width).T
    both = parts[0]
    for k in range(1, nlag):
        both = both + parts[k]
    powers = lax.broadcasted_iota(jnp.int32, (VECTORS, width), 0)
    total_row = jnp.zeros((1, width), jnp.float32)
    proj_lanes = jnp.zeros((VECTORS, width), jnp.float32)
    near = {}
    for s in range(nblk):
        deg = both[s : s + 1]
        bits = jnp.broadcast_to(both[nblk + s : nblk + s + 1].astype(jnp.int32), (VECTORS, width))
        start = (lax.shift_right_logical(bits, powers) & 1).astype(jnp.float32)
        total_row = total_row + deg
        proj_lanes = proj_lanes + start * jnp.sqrt(deg)
        if s in (0, 1, nblk - 1):
            near[s] = (start, lax.rsqrt(deg), jnp.sqrt(deg))
    total = jnp.sum(total_row, axis=1, keepdims=True)
    projection = jnp.sum(proj_lanes, axis=1, keepdims=True)
    order = (1, 0, nblk - 1)
    inverses = [near[s][1] for s in order]
    vectors = [near[s][0] for s in order]
    inverse, root = near[0][1], near[0][2]
    sub = lax.broadcasted_iota(jnp.int32, (VECTORS, width), 0)
    lane = lax.broadcasted_iota(jnp.int32, (VECTORS, width), 1)

    band = jnp.concatenate([before, centre, after], 0)

    def iterate(it, carry):
        projection, vectors = carry[0], carry[1:]
        scaled = jnp.concatenate([v * inv for v, inv in zip(vectors, inverses)], 1)
        applied = jnp.dot(scaled, band, precision=HIGHEST, preferred_element_type=jnp.float32)
        deflated = applied * inverse - root * (projection / total)
        yn[it, 0] = deflated
        copies = [
            remote(
                yn.at[it, 0],
                yn.at[it, slot],
                yn_send.at[it, slot],
                yn_recv.at[it, slot],
                block_at(step),
                me,
            )
            for slot, step in ((1, 1), (2, -1))
        ]
        for copy in copies:
            copy.start()
        gram = lax.dot_general(
            deflated,
            deflated,
            (((1,), (1,)), ((), ())),
            precision=HIGHEST,
            preferred_element_type=jnp.float32,
        )
        carried = jnp.sum(deflated * root, axis=1, keepdims=True)
        wide = jnp.concatenate([gram, jnp.zeros((VECTORS, width - VECTORS), jnp.float32)], 1)
        gm[it, 0] = jnp.where(lane == VECTORS, carried, wide)
        gm_copies = [
            remote(
                gm.at[it, 0],
                gm.at[it, s],
                gm_send.at[it, s],
                gm_recv.at[it, s],
                block_at(s),
                me,
            )
            for s in range(1, nblk)
        ]
        for copy in gm_copies:
            copy.start()
        for copy in gm_copies + copies:
            copy.wait()
        table = gm[it, 0]
        for s in range(1, nblk):
            table = table + gm[it, s]
        table = jnp.where(lane < VECTORS, table / events, table)
        tiles = [table, yn[it, 1], deflated, yn[it, 2]]
        for k in range(VECTORS):
            column = jnp.broadcast_to(tiles[0][:, k : k + 1], (VECTORS, width))
            r = lax.rsqrt(column[k : k + 1])
            factor = jnp.where(sub > k, column * r, 0.0)
            updated = []
            for tile in tiles:
                pivot = tile[k : k + 1] * r
                updated.append(jnp.where(sub == k, pivot, tile - factor * pivot))
            tiles = updated
        return (tiles[0][:, VECTORS : VECTORS + 1], *tiles[1:])

    final = lax.fori_loop(0, ITERS, iterate, (projection, *vectors))

    result = jnp.zeros((VECTORS, own), jnp.float32)
    for k in range(nlag):
        result = jnp.where(me == k, final[2][:, k * own : (k + 1) * own], result)
    out_ref[...] = result


def local(nblk, nlag, seismograms, onset_shift, start_bits):
    own = seismograms.shape[0]
    width = nlag * own
    events = own * nblk * nlag
    records = jnp.transpose(seismograms, (1, 0, 2)).reshape(COMPS * own, SAMPLES)
    f32, bf16 = jnp.float32, jnp.bfloat16
    dma = pltpu.SemaphoreType.DMA
    flat = COMPS * SAMPLES
    return pl.pallas_call(
        functools.partial(kernel, nblk, nlag, own, events),
        out_shape=jax.ShapeDtypeStruct((VECTORS, own), f32),
        in_specs=[pl.BlockSpec(memory_space=pltpu.HBM)] * 3,
        out_specs=pl.BlockSpec(memory_space=pltpu.VMEM),
        scratch_shapes=[
            pltpu.VMEM((COMPS * own, SAMPLES), f32),
            pltpu.VMEM((1, own), jnp.int32),
            pltpu.VMEM((1, own), jnp.int32),
            pltpu.VMEM((nlag, own, flat), bf16),
            pltpu.VMEM((own, flat), bf16),
            pltpu.VMEM((own, COMPS * PADDED), PAD_DTYPE),
            pltpu.VMEM((LAGS * own, flat), bf16),
            pltpu.VMEM((LAGS * own, flat), bf16),
            pltpu.VMEM((flat, width), bf16),
            pltpu.VMEM((2, nlag, own, width), f32),
            pltpu.VMEM((nlag, own, width), f32),
            pltpu.VMEM((nlag, 2 * nblk, width), f32),
            pltpu.VMEM((nblk, 8, width), f32),
            pltpu.VMEM((ITERS, 3, VECTORS, width), f32),
            pltpu.VMEM((ITERS, nblk, VECTORS, width), f32),
            dma((3,)),
            dma((6,)),
            dma((6,)),
            dma((nlag,)),
            dma((nlag,)),
            dma((2, nlag)),
            dma((2, nlag)),
            dma((nlag,)),
            dma((nlag,)),
            dma((nblk,)),
            dma((nblk,)),
            dma((ITERS, 3)),
            dma((ITERS, 3)),
            dma((ITERS, nblk)),
            dma((ITERS, nblk)),
        ],
        compiler_params=pltpu.CompilerParams(
            collective_id=0, has_side_effects=True, vmem_limit_bytes=50 * 1024 * 1024
        ),
    )(records, onset_shift[None, :], start_bits[None, :])


PAD_DTYPE = jnp.float32


def solution(mesh):
    spec = P(("blk", "lag"))
    return jax.shard_map(
        functools.partial(local, mesh.shape["blk"], mesh.shape["lag"]),
        mesh=mesh,
        in_specs=(P(("blk", "lag"), None, None), spec, spec),
        out_specs=P(None, ("blk", "lag")),
        check_vma=False,
    )
```
